512 devices in a mesh: dp: 4 (over x_hi, core), seq: 128 (over x_lo, y, z).
Axes of the slice: x: 4 (x_hi: 2, x_lo: 2; x = x_hi * 2 + x_lo), y: 4, z: 16, core: 2. Of those that a mesh axis runs over, the one named last changes fastest.
Arguments:
- tokens: bfloat16 [4, 128, 512, 768], P('dp', 'seq'), may hold values from -6 to 6
- left_factor: bfloat16 [512, 512], replicated, may hold values from -0.25 to 0.25
- right_factor: bfloat16 [128, 128], replicated, may hold values from -0.5 to 0.5
- gate_kernel: float32 [128, 512], P(None, 'seq'), may hold values from 0.5 to 2
- out_grad: bfloat16 [4, 128, 512, 768], P('dp', 'seq'), may hold values from -6 to 6
Outputs:
- mixed_out: bfloat16 [4, 128, 512, 768], P('dp', 'seq')
- tokens_grad: bfloat16 [4, 128, 512, 768], P('dp', 'seq')
- left_grad: float32 [512, 512], replicated
- right_grad: float32 [128, 128], replicated
- kernel_grad: float32 [128, 512], P(None, 'seq')
The draws below stay inside these ranges and needn't reach their ends.
All inputs are finite; a program needn't handle non-finite values.
Results may differ from the reference program's by a relative error of at most 0.0057.
Values may be sent and summed in bfloat16 or wider, within the bound.
A program may use at most 64 MiB of HBM per device.

```python
import math
import jax
import jax.numpy as jnp
from jax import lax

D = 768
S2 = 512
S1 = 128
BATCH = 4


def block_levels(own_key, extent, cuts, low, top_value):
    def one(position, parts):
        steps = jax.random.uniform(jax.random.fold_in(jax.random.fold_in(own_key, 6), position), (parts,), jnp.float32, low / len(cuts), top_value / len(cuts))
        return jnp.repeat(jnp.exp(steps), extent[position] // parts).reshape((-1,) + (1,) * (len(extent) - position - 1))

    loudness = one(*cuts[0])
    for cut in cuts[1:]:
        loudness = loudness * one(*cut)
    return loudness


def centred(key, dims, deviation, most, split=(), dtype=jnp.bfloat16):
    drawn = jax.random.normal(key, dims, jnp.float32) * deviation
    if len(split) > 0:
        drawn = block_levels(key, dims, split, -0.22, 0.18) * drawn
    return jnp.clip(drawn, min=-most, max=most).astype(dtype)


def setup_inputs(seed: int = 0) -> dict:
    arg_keys = jax.random.split(jax.random.key(seed), 6)
    return {
        "tokens": centred(arg_keys[0], (BATCH, S1, S2, D), 1.0, 6.0, ((0, 4), (1, 128))),
        "left_factor": centred(arg_keys[1], (S2, S2), S2 ** -0.5, 0.25),
        "right_factor": centred(arg_keys[2], (S1, S1), S1 ** -0.5, 0.5),
        "gate_kernel": jnp.clip(0.5 + 1.5 * jax.random.uniform(arg_keys[3], (S1, S2), jnp.float32) ** block_levels(arg_keys[3], (S1, S2), ((1, 128),), -0.2, 0.2), 0.5, 2.0),
        "out_grad": centred(arg_keys[4], (BATCH, S1, S2, D), 1.0, 6.0, ((0, 4), (1, 128))),
    }


def reference(tokens, left_factor, right_factor, gate_kernel, out_grad):
    left_wide = left_factor.astype(jnp.float32)
    right_wide = right_factor.astype(jnp.float32)

    def one_sequence(pair):
        tokens_one, grad_one = pair
        tokens_wide = tokens_one.astype(jnp.float32)
        first = jnp.einsum('ij,kjd->kid', left_wide, tokens_wide).astype(jnp.bfloat16)
        first_wide = first.astype(jnp.float32)
        blended = jnp.einsum('ak,kid->aid', right_wide, first_wide)
        output = (gate_kernel[:, :, None] * blended).astype(jnp.bfloat16)
        grad_wide = grad_one.astype(jnp.float32)
        kernel_part = lax.optimization_barrier(jnp.sum(grad_wide * blended, axis=2))
        weighted = (gate_kernel[:, :, None] * grad_wide).astype(jnp.bfloat16)
        weighted_wide = weighted.astype(jnp.float32)
        right_part = jnp.einsum('aid,kid->ak', weighted_wide, first_wide)
        back = jnp.einsum('ak,aid->kid', right_wide, weighted_wide).astype(jnp.bfloat16)
        back_wide = back.astype(jnp.float32)
        grad_tokens = jnp.einsum('ij,kid->kjd', left_wide, back_wide).astype(jnp.bfloat16)
        left_part = jnp.einsum('kid,kjd->ij', back_wide, tokens_wide)
        return (output, grad_tokens, kernel_part, right_part, left_part)
    outputs, grads, kernel_parts, right_parts, left_parts = lax.map(one_sequence, (tokens, out_grad))
    kernel_grad = lax.optimization_barrier(jnp.sum(kernel_parts, axis=0)) / math.sqrt(BATCH * D)
    right_grad = lax.optimization_barrier(jnp.sum(right_parts, axis=0)) / math.sqrt(BATCH * S2 * D)
    left_grad = lax.optimization_barrier(jnp.sum(left_parts, axis=0)) / math.sqrt(BATCH * S1 * D)
    return (outputs, grads, left_grad, right_grad, kernel_grad)
```

```python
import math

import jax
import jax.numpy as jnp
from jax import lax
from jax.experimental import pallas as pl
from jax.experimental.pallas import tpu as pltpu
from jax.sharding import PartitionSpec as P

MESH = pl.DeviceIdType.MESH
BF16, F32 = jnp.bfloat16, jnp.float32
D, S2, S1, BATCH = 768, 512, 128, 4
NZ, NQ = 16, 8
ZROWS, QROWS = S2 // NZ, S2 // NQ
LANES = 256
ZORDER = [8, -7, 7, -6, 6, -5, 5, -4, 4, -3, 3, -2, 2, -1, 1]
LEFT_SCALE = 1.0 / math.sqrt(BATCH * S1 * D)
RIGHT_SCALE = 1.0 / math.sqrt(BATCH * S2 * D)
KERNEL_SCALE = 1.0 / math.sqrt(BATCH * D)


def dot(a, b, dims=((1,), (0,)), precision=None):
    return lax.dot_general(a, b, (dims, ((), ())), preferred_element_type=F32, precision=precision)


def iotas(rows, columns):
    return (
        lax.broadcasted_iota(jnp.int32, (rows, columns), 0),
        lax.broadcasted_iota(jnp.int32, (rows, columns), 1),
    )


def lane_tiles(body):
    def step(t, carry):
        body(pl.ds(pl.multiple_of(t * LANES, LANES), LANES))
        return carry

    lax.fori_loop(0, D // LANES, step, 0)


def kernel(
    tokens_hbm, left_ref, right_ref, gate_ref, grad_hbm,
    mixed_ref, tgrad_ref, lgrad_ref, rgrad_ref, kgrad_ref,
    tokens, grad_own, first, g1, g1p, g2, weighted, bo, b1, b1p, b2, f1, f1p, f2, blended, mo, m1, m1p,
    to_q, to_z, expand, mix, mix_t, gate_send, gate_mine, gate_col, ksum,
    left_local, left_mate, left_half, left_xy, right_local, right_mate, right_half, right_xy,
    z_send, z_recv, total, x_recv, piece,
    k_local, k_core, k_half, k_hi, k_total, k_home,
    load_sem, own_sem, z_ss, z_rs, q_ss, q_rs, r_ss, r_rs, rq_ss, rq_rs, rz_ss, rz_rs,
):
    dp, me = lax.axis_index("dp"), lax.axis_index("seq")
    z, q = lax.rem(me, NZ), lax.div(me, NZ)
    core, x_hi = lax.rem(dp, 2), lax.div(dp, 2)
    mate = (x_hi * 2 + (1 - core), me)
    across = ((1 - x_hi) * 2 + core, me)
    z_peers = [lax.rem(z + d + NZ, NZ) for d in ZORDER]
    q_peers = [lax.bitwise_xor(q, d) for d in range(1, NQ)]
    user = lax.rem(me, NQ) * NZ + lax.div(me, NQ)
    holder = z * NQ + q
    moves = user != me

    load_tokens = pltpu.make_async_copy(tokens_hbm, tokens, load_sem.at[0])
    load_tokens.start()
    barrier = pltpu.get_barrier_semaphore()
    for zz in z_peers:
        pl.semaphore_signal(barrier, inc=1, device_id=(dp, q * NZ + zz), device_id_type=MESH)
    for qq in q_peers:
        pl.semaphore_signal(barrier, inc=1, device_id=(dp, qq * NZ + z), device_id_type=MESH)
    pl.semaphore_signal(barrier, inc=1, device_id=mate, device_id_type=MESH)
    pl.semaphore_signal(barrier, inc=1, device_id=across, device_id_type=MESH)

    @pl.when(moves)
    def _():
        pl.semaphore_signal(barrier, inc=1, device_id=(dp, user), device_id_type=MESH)
        pl.semaphore_signal(barrier, inc=1, device_id=(dp, holder), device_id_type=MESH)

    pl.semaphore_wait(barrier, jnp.where(moves, NZ + NQ + 2, NZ + NQ))

    def send(src, dst, ss, rs, device):
        copy = pltpu.make_async_remote_copy(
            src_ref=src, dst_ref=dst, send_sem=ss, recv_sem=rs, device_id=device, device_id_type=MESH
        )
        copy.start()
        return copy

    def block(ref, index, rows):
        return ref.at[pl.ds(pl.multiple_of(index * rows, rows), rows)]

    def z_exchange(n, src, dst):
        own = pltpu.make_async_copy(block(src, z, ZROWS), block(dst, z, ZROWS), own_sem.at[n])
        own.start()
        return own, [
            send(block(src, zz, ZROWS), block(dst, z, ZROWS), z_ss.at[n, j], z_rs.at[n, j], (dp, q * NZ + zz))
            for j, zz in enumerate(z_peers)
        ]

    def q_exchange(n, src, dst):
        own = pltpu.make_async_copy(block(src, q, QROWS), block(dst, q, QROWS), own_sem.at[4 + n])
        own.start()
        return own, [
            send(block(src, qq, QROWS), block(dst, q, QROWS), q_ss.at[n, j], q_rs.at[n, j], (dp, qq * NZ + z))
            for j, qq in enumerate(q_peers)
        ]

    def arrive(exchange):
        exchange[0].wait()
        for copy in exchange[1]:
            copy.wait_recv()

    def sent(exchange):
        for copy in exchange[1]:
            copy.wait_send()

    gz = z_exchange(0, grad_hbm, g1)

    load_tokens.wait()

    def step_first(lanes):
        first[:, lanes] = dot(left_ref[...], tokens[:, lanes]).astype(BF16)

    lane_tiles(step_first)
    fz = z_exchange(1, first, f1)

    gate_send[...] = jnp.zeros((8, S1), F32)
    gate_send[0:4, :] = gate_ref[...]

    def move(src, dst, n, device):
        remote = pltpu.make_async_remote_copy(
            src_ref=src, dst_ref=dst, send_sem=r_ss.at[n], recv_sem=r_rs.at[n], device_id=device, device_id_type=MESH
        )
        local = pltpu.make_async_copy(src, dst, own_sem.at[8 + n])

        @pl.when(moves)
        def _():
            remote.start()

        @pl.when(jnp.logical_not(moves))
        def _():
            local.start()

        def finish():
            @pl.when(moves)
            def _():
                remote.wait()

            @pl.when(jnp.logical_not(moves))
            def _():
                local.wait()

        return finish

    gate_moved = move(gate_send, gate_mine, 0, (dp, user))

    r, c = iotas(S2, S2)
    to_q[...] = jnp.where((r // 4 % NZ) * ZROWS + (r // QROWS) * 4 + r % 4 == c, 1.0, 0.0).astype(BF16)
    to_z[...] = jnp.where((c // 4 % NZ) * ZROWS + (c // QROWS) * 4 + c % 4 == r, 1.0, 0.0).astype(BF16)
    re, ce = iotas(S2, S1)
    expand[...] = jnp.where(re // 4 == ce, 1.0, 0.0).astype(BF16)
    same = (r % 4 == c % 4).astype(F32)
    wide = dot(expand[...], right_ref[...]).astype(BF16)
    mix[...] = (dot(wide, expand[...], ((1,), (1,))) * same).astype(BF16)
    wide_t = dot(expand[...], right_ref[...], ((1,), (1,))).astype(BF16)
    mix_t[...] = (dot(wide_t, expand[...], ((1,), (1,))) * same).astype(BF16)
    gate_moved()
    pick = jnp.where(re % 4 == ce, 1.0, 0.0)
    gates = jnp.concatenate([gate_mine[...], jnp.zeros((S1 - 8, S1), F32)], axis=0)
    spread = dot(expand[...].astype(F32), gates, ((1,), (1,)), lax.Precision.HIGHEST)
    gate_col[...] = jnp.broadcast_to(jnp.sum(spread * pick, axis=1, keepdims=True), (S2, S1))

    def reorder(matrix, src, dst):
        def step(lanes):
            dst[:, lanes] = dot(matrix[...], src[:, lanes]).astype(BF16)

        lane_tiles(step)

    arrive(gz)
    reorder(to_q, g1, g1p)
    gq = q_exchange(0, g1p, g2)
    arrive(gq)

    def step_back(lanes):
        gate = gate_col[:, 0:1]
        w = (gate * g2[:, lanes].astype(F32)).astype(BF16)
        weighted[:, lanes] = w
        bo[:, lanes] = dot(mix_t[...], w).astype(BF16)

    lane_tiles(step_back)
    bq = q_exchange(1, bo, b1)
    arrive(bq)
    reorder(to_z, b1, b1p)
    bz = z_exchange(2, b1p, b2)

    arrive(fz)
    reorder(to_q, f1, f1p)
    fq = q_exchange(2, f1p, f2)
    arrive(fq)

    def step_mixed(lanes):
        value = dot(mix[...], f2[:, lanes])
        blended[:, lanes] = value
        mo[:, lanes] = (gate_col[:, 0:1] * value).astype(BF16)

    lane_tiles(step_mixed)
    mq = q_exchange(3, mo, m1)
    arrive(mq)
    reorder(to_z, m1, m1p)
    mz = z_exchange(3, m1p, mixed_ref)

    ksum[...] = jnp.zeros((S2, S1), F32)

    def step_kernel(lanes):
        rows = jnp.sum(g2[:, lanes].astype(F32) * blended[:, lanes], axis=1, keepdims=True)
        ksum[...] += jnp.broadcast_to(rows, (S2, S1))

    lane_tiles(step_kernel)
    by_block = dot(expand[...].astype(F32), ksum[...] * pick, ((0,), (0,)), lax.Precision.HIGHEST)
    k_local[...] = by_block.T[0:8, :]
    k1 = send(k_local, k_core, r_ss.at[1], r_rs.at[1], mate)

    left_local[...] = jnp.zeros((S2, S2), F32)

    def step_right(lanes):
        left_local[...] += dot(weighted[:, lanes], f2[:, lanes], ((1,), (1,)))

    lane_tiles(step_right)
    pairs = left_local[...] * same
    halves = dot(expand[...].astype(F32), pairs, ((0,), (0,)), lax.Precision.HIGHEST)
    right_local[...] = dot(halves, expand[...].astype(F32), ((1,), (0,)), lax.Precision.HIGHEST)

    k1.wait()
    k_half[...] = k_local[...] + k_core[...]
    k2 = send(k_half, k_hi, r_ss.at[2], r_rs.at[2], across)
    k2.wait()
    k_total[...] = (k_half[...] + k_hi[...]) * KERNEL_SCALE
    kernel_moved = move(k_total, k_home, 3, (dp, holder))

    arrive(bz)
    left_local[...] = jnp.zeros((S2, S2), F32)

    def step_left(lanes):
        left_local[...] += dot(b2[:, lanes], tokens[:, lanes], ((1,), (1,)))

    lane_tiles(step_left)

    half, quarter = S2 // 2, S1 // 2
    c1 = send(block(left_local, 1 - core, half), left_mate, r_ss.at[4], r_rs.at[4], mate)
    c2 = send(block(right_local, 1 - core, quarter), right_mate, r_ss.at[5], r_rs.at[5], mate)

    def step_tokens(lanes):
        tgrad_ref[:, lanes] = dot(left_ref[...], b2[:, lanes], ((0,), (0,))).astype(BF16)

    lane_tiles(step_tokens)
    c1.wait()
    c2.wait()
    left_half[...] = left_local[pl.ds(pl.multiple_of(core * half, half), half), :] + left_mate[...]
    right_half[...] = right_local[pl.ds(pl.multiple_of(core * quarter, quarter), quarter), :] + right_mate[...]
    rows_l, rows_r = half // NQ, quarter // NQ
    xy = []
    for j, qq in enumerate(q_peers):
        there = (dp, qq * NZ + z)
        xy.append(send(block(left_half, qq, rows_l), left_xy.at[j], rq_ss.at[0, j], rq_rs.at[0, j], there))
        xy.append(send(block(right_half, qq, rows_r), right_xy.at[j], rq_ss.at[1, j], rq_rs.at[1, j], there))
    sum_l = left_half[pl.ds(pl.multiple_of(q * rows_l, rows_l), rows_l), :]
    sum_r = right_half[pl.ds(pl.multiple_of(q * rows_r, rows_r), rows_r), :]
    for copy in xy:
        copy.wait()
    for j in range(NQ - 1):
        sum_l = sum_l + left_xy[j]
        sum_r = sum_r + right_xy[j]
    for n in range(NZ):
        z_send[n, 0:8, :] = sum_l[n // 4 * 8 : n // 4 * 8 + 8, n % 4 * 128 : n % 4 * 128 + 128]
        z_send[n, 8:16, :] = sum_r
    own_tile = pltpu.make_async_copy(z_send.at[z], z_recv.at[z], own_sem.at[12])
    own_tile.start()
    zs = [
        send(z_send.at[zz], z_recv.at[z], rz_ss.at[0, j], rz_rs.at[0, j], (dp, q * NZ + zz))
        for j, zz in enumerate(z_peers)
    ]
    own_tile.wait()
    for copy in zs:
        copy.wait()
    tiles = z_recv[0]
    for n in range(1, NZ):
        tiles = tiles + z_recv[n]
    total[...] = tiles
    xs = send(total, x_recv, r_ss.at[6], r_rs.at[6], across)
    xs.wait()
    whole = total[...] + x_recv[...]
    piece[...] = whole[0:8, :] * LEFT_SCALE
    first_row = core * half + q * rows_l
    rgrad_ref[pl.ds(pl.multiple_of(core * quarter + q * rows_r, 8), 8), :] = whole[8:16, :] * RIGHT_SCALE
    spot = lgrad_ref.at[
        pl.ds(pl.multiple_of(first_row + z // 4 * 8, 8), 8), pl.ds(pl.multiple_of(z % 4 * 128, 128), 128)
    ]
    own_piece = pltpu.make_async_copy(piece, spot, own_sem.at[13])
    own_piece.start()
    zg = [
        send(piece, spot, rz_ss.at[1, j], rz_rs.at[1, j], (dp, q * NZ + zz)) for j, zz in enumerate(z_peers)
    ]
    own_piece.wait()
    for copy in zg:
        copy.wait()
    part_l = lgrad_ref.at[pl.ds(pl.multiple_of(first_row, rows_l), rows_l)]
    part_r = rgrad_ref.at[pl.ds(pl.multiple_of(core * quarter + q * rows_r, rows_r), rows_r)]
    xg = []
    for j, qq in enumerate(q_peers):
        there = (dp, qq * NZ + z)
        xg.append(send(part_l, part_l, rq_ss.at[2, j], rq_rs.at[2, j], there))
        xg.append(send(part_r, part_r, rq_ss.at[3, j], rq_rs.at[3, j], there))
    for copy in xg:
        copy.wait()
    half_l, half_r = block(lgrad_ref, core, half), block(rgrad_ref, core, quarter)
    h1 = send(half_l, half_l, r_ss.at[7], r_rs.at[7], mate)
    h2 = send(half_r, half_r, r_ss.at[8], r_rs.at[8], mate)
    kernel_moved()
    kgrad_ref[...] = k_home[0:4, :]
    h1.wait()
    h2.wait()

    arrive(mz)
    for exchange in (gz, fz, gq, bq, bz, fq, mq, mz):
        sent(exchange)


def on_device(tokens, left_factor, right_factor, gate_kernel, out_grad):
    vmem = pl.BlockSpec(memory_space=pltpu.VMEM)
    hbm = pl.BlockSpec(memory_space=pl.ANY)
    plane = pltpu.VMEM((S2, D), BF16)
    square = pltpu.VMEM((S2, S2), BF16)
    tile = pltpu.VMEM((8, S1), F32)
    half, quarter = S2 // 2, S1 // 2
    dma = pltpu.SemaphoreType.DMA
    mixed, tgrad, lgrad, rgrad, kgrad = pl.pallas_call(
        kernel,
        name="monarch",
        out_shape=(
            jax.ShapeDtypeStruct((S2, D), BF16),
            jax.ShapeDtypeStruct((S2, D), BF16),
            jax.ShapeDtypeStruct((S2, S2), F32),
            jax.ShapeDtypeStruct((S1, S1), F32),
            jax.ShapeDtypeStruct((4, S1), F32),
        ),
        in_specs=[hbm, vmem, vmem, vmem, hbm],
        out_specs=(vmem,) * 5,
        scratch_shapes=[
            *[plane] * 14,
            pltpu.VMEM((S2, D), F32),
            *[plane] * 3,
            square, square, pltpu.VMEM((S2, S1), BF16), square, square,
            tile, tile, pltpu.VMEM((S2, S1), F32), pltpu.VMEM((S2, S1), F32),
            pltpu.VMEM((S2, S2), F32), pltpu.VMEM((half, S2), F32), pltpu.VMEM((half, S2), F32),
            pltpu.VMEM((NQ - 1, half // NQ, S2), F32),
            pltpu.VMEM((S1, S1), F32), pltpu.VMEM((quarter, S1), F32), pltpu.VMEM((quarter, S1), F32),
            pltpu.VMEM((NQ - 1, quarter // NQ, S1), F32),
            pltpu.VMEM((NZ, 16, S1), F32), pltpu.VMEM((NZ, 16, S1), F32),
            pltpu.VMEM((16, S1), F32), pltpu.VMEM((16, S1), F32), tile,
            *[tile] * 6,
            dma((1,)), dma((14,)), dma((4, NZ - 1)), dma((4, NZ - 1)), dma((4, NQ - 1)), dma((4, NQ - 1)),
            dma((9,)), dma((9,)), dma((4, NQ - 1)), dma((4, NQ - 1)), dma((2, NZ - 1)), dma((2, NZ - 1)),
        ],
        compiler_params=pltpu.CompilerParams(
            collective_id=0, has_side_effects=True, vmem_limit_bytes=56 * 1024 * 1024
        ),
    )(tokens.reshape(S2, D), left_factor, right_factor, gate_kernel.T, out_grad.reshape(S2, D))
    return mixed.reshape(tokens.shape), tgrad.reshape(tokens.shape), lgrad, rgrad, kgrad.T


def solution(mesh):
    blocks = P("dp", "seq", None, None)
    return jax.shard_map(
        on_device,
        mesh=mesh,
        in_specs=(blocks, P(), P(), P(None, "seq"), blocks),
        out_specs=(blocks, blocks, P(), P(), P(None, "seq")),
        check_vma=False,
    )
```

```python
import math

import jax
import jax.numpy as jnp
from jax import lax
from jax.experimental import pallas as pl
from jax.experimental.pallas import tpu as pltpu
from jax.sharding import PartitionSpec as P

MESH = pl.DeviceIdType.MESH
BF16, F32 = jnp.bfloat16, jnp.float32
D, S2, S1, BATCH = 768, 512, 128, 4
NZ, NQ, NC = 16, 8, 16
ZROWS, QROWS = S2 // NZ, S2 // NQ
LANES = 256
ZORDER = [8, -7, 7, -6, 6, -5, 5, -4, 4, -3, 3, -2, 2, -1, 1]
MPARTS = [[8, -7, 7], [-6, 6], [-5, 5, -4, 4, -3, 3, -2, 2, -1, 1]]
KEEP_PARTS = 4
VMEM_LIMIT = 56 * 1024 * 1024
LEFT_SCALE = 1.0 / math.sqrt(BATCH * S1 * D)
RIGHT_SCALE = 1.0 / math.sqrt(BATCH * S2 * D)
KERNEL_SCALE = 1.0 / math.sqrt(BATCH * D)


def dot(a, b, dims=((1,), (0,)), precision=None):
    return lax.dot_general(a, b, (dims, ((), ())), preferred_element_type=F32, precision=precision)


def iotas(rows, columns):
    return (
        lax.broadcasted_iota(jnp.int32, (rows, columns), 0),
        lax.broadcasted_iota(jnp.int32, (rows, columns), 1),
    )


def lane_tiles(body):
    def step(t, carry):
        body(pl.ds(pl.multiple_of(t * LANES, LANES), LANES))
        return carry

    lax.fori_loop(0, D // LANES, step, 0)


def kernel(
    tokens_hbm, left_hbm, right_hbm, gate_hbm, grad_hbm,
    mixed_ref, tgrad_ref, lgrad_ref, rgrad_ref, kgrad_ref,
    tokens, left_ref, right_ref, first, g1, g1p, g2, weighted, bo, b1, b1p, b2, f1, f1p, f2, blended, mo, m1, m1p, tgrad,
    to_q, to_z, expand, mix, mix_t, gate_mine, gate_col, ksum,
    left_give, left_mate, left_half, left_xy, z_send, z_recv, piece,
    lgrad, pairs, right_local, right_xy, right_sum, right_mate, right_half, right_z, right_piece, rgrad,
    k_local, k_core, k_half, k_hi, k_total, k_home,
    load_sem, own_sem, z_ss, z_rs, q_ss, q_rs, s_ss, s_rs, x_ss, x_rs,
):
    dp, me = lax.axis_index("dp"), lax.axis_index("seq")
    z, q = lax.rem(me, NZ), lax.div(me, NZ)
    core, x_hi = lax.rem(dp, 2), lax.div(dp, 2)
    chip = x_hi * NQ + q
    mate = (x_hi * 2 + (1 - core), me)
    across = ((1 - x_hi) * 2 + core, me)
    z_peers = [lax.rem(z + d + NZ, NZ) for d in ZORDER]
    q_peers = [lax.bitwise_xor(q, d) for d in range(1, NQ)]
    chip_peers = [lax.bitwise_xor(chip, d) for d in range(1, NC)]

    def along_z(zz):
        return (dp, q * NZ + zz)

    def along_q(qq):
        return (dp, qq * NZ + z)

    def at_chip(cc):
        return (lax.div(cc, NQ) * 2 + core, lax.rem(cc, NQ) * NZ + z)

    user = lax.rem(me, NQ) * NZ + lax.div(me, NQ)
    holder = z * NQ + q
    moves = user != me

    barrier = pltpu.get_barrier_semaphore()

    def greet(device):
        pl.semaphore_signal(barrier, inc=1, device_id=device, device_id_type=MESH)

    for zz in z_peers:
        greet(along_z(zz))

    @pl.when(moves)
    def _():
        greet((dp, user))
        greet((dp, holder))

    for cc in chip_peers:
        greet(at_chip(cc))
    greet(mate)
    loads = [
        pltpu.make_async_copy(src, dst, load_sem.at[n])
        for n, (src, dst) in enumerate([(tokens_hbm, tokens), (left_hbm, left_ref), (right_hbm, right_ref)])
    ]
    for load in loads:
        load.start()
    pl.semaphore_wait(barrier, jnp.where(moves, NZ + NC + 1, NZ + NC - 1))

    def send(src, dst, ss, rs, device):
        copy = pltpu.make_async_remote_copy(
            src_ref=src, dst_ref=dst, send_sem=ss, recv_sem=rs, device_id=device, device_id_type=MESH
        )
        copy.start()
        return copy

    def block(ref, index, rows):
        return ref.at[pl.ds(pl.multiple_of(index * rows, rows), rows)]

    def z_part(n, src, dst, distances):
        for d in distances:
            zz = z_peers[ZORDER.index(d)]
            send(block(src, zz, ZROWS), block(dst, z, ZROWS), z_ss.at[n], z_rs.at[n], along_z(zz))

    def z_own(n, src, dst):
        own = pltpu.make_async_copy(block(src, z, ZROWS), block(dst, z, ZROWS), own_sem.at[n])
        own.start()
        return own

    def q_exchange(n, src, dst):
        own = pltpu.make_async_copy(block(src, q, QROWS), block(dst, q, QROWS), own_sem.at[4 + n])
        own.start()
        for qq in q_peers:
            send(block(src, qq, QROWS), block(dst, q, QROWS), q_ss.at[n], q_rs.at[n], along_q(qq))
        return own

    def bytes_of(ref, sem):
        pltpu.make_async_copy(ref, ref, sem).wait()

    def z_bytes(ref, sem):
        bytes_of(ref.at[pl.ds(0, S2 - ZROWS)], sem)

    def q_bytes(ref, sem):
        bytes_of(ref.at[pl.ds(0, S2 - QROWS)], sem)

    def z_arrive(n, own, dst):
        own.wait()
        z_bytes(dst, z_rs.at[n])

    def q_arrive(n, own, dst):
        own.wait()
        q_bytes(dst, q_rs.at[n])

    def move(src, dst, n, device):
        remote = pltpu.make_async_remote_copy(
            src_ref=src, dst_ref=dst, send_sem=s_ss.at[n], recv_sem=s_rs.at[n], device_id=device, device_id_type=MESH
        )
        local = pltpu.make_async_copy(src, dst, own_sem.at[8 + n])

        @pl.when(moves)
        def _():
            remote.start()

        @pl.when(jnp.logical_not(moves))
        def _():
            local.start()

        def finish():
            @pl.when(moves)
            def _():
                remote.wait()

            @pl.when(jnp.logical_not(moves))
            def _():
                local.wait()

        return finish

    gate_moved = move(gate_hbm, gate_mine, 0, (dp, user))
    z_part(0, grad_hbm, g1, ZORDER)
    g_own = z_own(0, grad_hbm, g1)

    loads[0].wait()
    loads[1].wait()

    def step_first(lanes):
        first[:, lanes] = dot(left_ref[...], tokens[:, lanes]).astype(BF16)

    lane_tiles(step_first)

    r, c = iotas(S2, S2)
    to_q[...] = jnp.where((r // 4 % NZ) * ZROWS + (r // QROWS) * 4 + r % 4 == c, 1.0, 0.0).astype(BF16)
    to_z[...] = jnp.where((c // 4 % NZ) * ZROWS + (c // QROWS) * 4 + c % 4 == r, 1.0, 0.0).astype(BF16)
    re, ce = iotas(S2, S1)
    expand[...] = jnp.where(re // 4 == ce, 1.0, 0.0).astype(BF16)
    same = (r % 4 == c % 4).astype(F32)
    loads[2].wait()
    wide = dot(expand[...], right_ref[...]).astype(BF16)
    mix[...] = (dot(wide, expand[...], ((1,), (1,))) * same).astype(BF16)
    wide_t = dot(expand[...], right_ref[...], ((1,), (1,))).astype(BF16)
    mix_t[...] = (dot(wide_t, expand[...], ((1,), (1,))) * same).astype(BF16)
    gate_moved()
    pick = jnp.where(re % 4 == ce, 1.0, 0.0)
    gates = jnp.concatenate([gate_mine[...], jnp.zeros((S1 - 4, S1), F32)], axis=0)
    z_bytes(g1, z_ss.at[0])
    f_own = z_own(1, first, f1)
    z_part(1, first, f1, ZORDER)
    spread = dot(expand[...].astype(F32), gates, ((1,), (1,)), lax.Precision.HIGHEST)
    gate_col[...] = jnp.broadcast_to(jnp.sum(spread * pick, axis=1, keepdims=True), (S2, S1))

    def reorder(matrix, src, dst):
        def step(lanes):
            dst[:, lanes] = dot(matrix[...], src[:, lanes]).astype(BF16)

        lane_tiles(step)

    z_arrive(0, g_own, g1)
    reorder(to_q, g1, g1p)
    q_arrive(0, q_exchange(0, g1p, g2), g2)

    def step_back(lanes):
        w = (gate_col[:, 0:1] * g2[:, lanes].astype(F32)).astype(BF16)
        weighted[:, lanes] = w
        bo[:, lanes] = dot(mix_t[...], w).astype(BF16)

    lane_tiles(step_back)
    q_arrive(1, q_exchange(1, bo, b1), b1)
    reorder(to_z, b1, b1p)
    z_part(2, b1p, b2, ZORDER)
    b_own = z_own(2, b1p, b2)

    z_arrive(1, f_own, f1)
    reorder(to_q, f1, f1p)
    q_arrive(2, q_exchange(2, f1p, f2), f2)

    def step_mixed(lanes):
        value = dot(mix[...], f2[:, lanes])
        blended[:, lanes] = value
        mo[:, lanes] = (gate_col[:, 0:1] * value).astype(BF16)

    lane_tiles(step_mixed)
    mq_own = q_exchange(3, mo, m1)

    ksum[...] = jnp.zeros((S2, S1), F32)

    def step_kernel(lanes):
        rows = jnp.sum(g2[:, lanes].astype(F32) * blended[:, lanes], axis=1, keepdims=True)
        ksum[...] += jnp.broadcast_to(rows, (S2, S1))

    lane_tiles(step_kernel)
    by_block = dot(expand[...].astype(F32), ksum[...] * pick, ((0,), (0,)), lax.Precision.HIGHEST)
    k_local[...] = by_block.T[0:4, :]
    k1 = send(k_local, k_core, s_ss.at[1], s_rs.at[1], mate)

    pairs[...] = jnp.zeros((S2, S2), F32)

    def step_right(lanes):
        pairs[...] += dot(weighted[:, lanes], f2[:, lanes], ((1,), (1,)))

    lane_tiles(step_right)
    halves = dot(expand[...].astype(F32), pairs[...] * same, ((0,), (0,)), lax.Precision.HIGHEST)
    right_local[...] = dot(halves, expand[...].astype(F32), ((1,), (0,)), lax.Precision.HIGHEST)
    for j, cc in enumerate(chip_peers):
        send(block(right_local, cc, 8), right_xy.at[j], s_ss.at[6], s_rs.at[6], at_chip(cc))
    k1.wait()
    k_half[...] = k_local[...] + k_core[...]
    k2 = send(k_half, k_hi, s_ss.at[2], s_rs.at[2], across)

    q_arrive(3, mq_own, m1)
    reorder(to_z, m1, m1p)
    k2.wait()
    k_total[...] = (k_half[...] + k_hi[...]) * KERNEL_SCALE
    kernel_moved = move(k_total, k_home, 3, (dp, holder))
    sum_r = right_local[pl.ds(pl.multiple_of(chip * 8, 8), 8), :]
    bytes_of(right_xy, s_ss.at[6])
    bytes_of(right_xy, s_rs.at[6])
    for j in range(NC - 1):
        sum_r = sum_r + right_xy[j]
    right_sum[...] = sum_r
    rm = send(right_sum, right_mate, s_ss.at[4], s_rs.at[4], mate)
    m_own = z_own(3, m1p, mixed_ref)
    rm.wait()
    right_half[...] = right_sum[...] + right_mate[...]
    right_z[z] = right_half[...]
    for zz in z_peers:
        send(right_half, right_z.at[z], s_ss.at[7], s_rs.at[7], along_z(zz))
    z_bytes(b2, z_ss.at[2])
    z_part(3, m1p, mixed_ref, MPARTS[0])

    z_arrive(2, b_own, b2)
    half = S2 // 2
    rows_l = half // NC

    def left_rows(index):
        rows = b2[pl.ds(pl.multiple_of(index * half, half), half), :]
        return dot(rows, tokens[...], ((1,), (1,)))

    left_give[...] = left_rows(1 - core)
    c1 = send(left_give, left_mate, s_ss.at[5], s_rs.at[5], mate)
    left_half[...] = left_rows(core)
    c1.wait()
    left_half[...] += left_mate[...]
    for j, cc in enumerate(chip_peers):
        send(block(left_half, cc, rows_l), left_xy.at[j], s_ss.at[8], s_rs.at[8], at_chip(cc))

    def step_tokens(lanes):
        tgrad[:, lanes] = dot(left_ref[...], b2[:, lanes], ((0,), (0,))).astype(BF16)

    lane_tiles(step_tokens)
    save_tokens = pltpu.make_async_copy(tgrad, tgrad_ref, own_sem.at[12])
    save_tokens.start()

    sum_l = left_half[pl.ds(pl.multiple_of(chip * rows_l, rows_l), rows_l), :]
    bytes_of(left_xy, s_ss.at[8])
    bytes_of(left_xy, s_rs.at[8])
    for j in range(NC - 1):
        sum_l = sum_l + left_xy[j]
    for n in range(8):
        z_send[n] = sum_l[n // 4 * 8 : n // 4 * 8 + 8, n % 4 * 128 : n % 4 * 128 + 128]
    z_recv[z] = z_send[lax.rem(z, 8)]
    for zz in z_peers:
        send(z_send.at[lax.rem(zz, 8)], z_recv.at[z], s_ss.at[9], s_rs.at[9], along_z(zz))
    z_part(3, m1p, mixed_ref, MPARTS[1])

    z_tiles = right_z.at[pl.ds(0, NZ - 1)]
    bytes_of(z_tiles, s_ss.at[7])
    bytes_of(z_tiles, s_rs.at[7])
    whole_r = right_z[0]
    for n in range(1, NZ):
        whole_r = whole_r + right_z[n]
    right_piece[...] = whole_r * RIGHT_SCALE
    rgrad[pl.ds(pl.multiple_of(chip * 8, 8), 8), :] = right_piece[...]
    for cc in chip_peers:
        send(right_piece, block(rgrad, chip, 8), s_ss.at[10], s_rs.at[10], at_chip(cc))

    bytes_of(z_tiles, s_ss.at[9])
    bytes_of(z_tiles, s_rs.at[9])
    whole_l = z_recv[0]
    for n in range(1, NZ):
        whole_l = whole_l + z_recv[n]
    piece[...] = whole_l * LEFT_SCALE
    first_row = core * half + chip * rows_l
    part = lax.rem(z, 8)
    spot_l = lgrad.at[
        pl.ds(pl.multiple_of(first_row + part // 4 * 8, 8), 8), pl.ds(pl.multiple_of(part % 4 * 128, 128), 128)
    ]
    own_l = pltpu.make_async_copy(piece, spot_l, own_sem.at[13])
    own_l.start()
    for d in (-4, 3, -3, 2, -2, 1, -1):
        zz = z_peers[ZORDER.index(d)]
        send(piece, spot_l, s_ss.at[11], s_rs.at[11], along_z(zz))
    z_part(3, m1p, mixed_ref, MPARTS[2])
    own_l.wait()
    seven = z_recv.at[pl.ds(0, 7)]
    bytes_of(seven, s_ss.at[11])
    bytes_of(seven, s_rs.at[11])

    def part_l(which, cc):
        return lgrad.at[pl.ds(pl.multiple_of(which * half + cc * rows_l, rows_l), rows_l)]

    mine = part_l(core, chip)
    lx = [send(mine, mine, x_ss.at[0], x_rs.at[j], at_chip(cc)) for j, cc in enumerate(chip_peers)]
    send(mine, mine, x_ss.at[1], s_rs.at[12], mate)
    for j, cc in enumerate(chip_peers):
        lx[j].wait_recv()
        send(part_l(core, cc), part_l(core, cc), x_ss.at[1], s_rs.at[12], mate)
    kernel_moved()
    bytes_of(right_xy, s_ss.at[10])
    bytes_of(right_xy, s_rs.at[10])
    saves = [
        pltpu.make_async_copy(src, dst, own_sem.at[14 + n])
        for n, (src, dst) in enumerate([(k_home, kgrad_ref), (rgrad, rgrad_ref), (lgrad, lgrad_ref)])
    ]
    saves[0].start()
    saves[1].start()
    bytes_of(left_xy, x_ss.at[0])
    bytes_of(lgrad.at[pl.ds(0, half)], x_ss.at[1])
    bytes_of(lgrad.at[pl.ds(0, half)], s_rs.at[12])
    saves[2].start()
    save_tokens.wait()
    z_bytes(f1, z_ss.at[1])
    z_bytes(m1p, z_ss.at[3])
    for n, buffer in enumerate([g2, b1, f2, m1]):
        q_bytes(buffer, q_ss.at[n])
    z_arrive(3, m_own, m1p)
    for save in saves:
        save.wait()


def keep(*refs):
    pieces = []
    for n in range(5):
        rows = refs[n].shape[0]
        step = max(rows // KEEP_PARTS, 4) if rows == S2 else rows
        pieces += [(n, at, step) for at in range(0, rows, step)]
    load_sem, save_sem = refs[15], refs[16]
    loads, saves = [], []
    for i, (n, at, step) in enumerate(pieces):
        spot = pl.ds(at, step)
        loads.append(pltpu.make_async_copy(refs[n].at[spot], refs[10 + n].at[spot], load_sem.at[i]))
        saves.append(pltpu.make_async_copy(refs[10 + n].at[spot], refs[5 + n].at[spot], save_sem.at[i]))
        loads[-1].start()
    for load, save in zip(loads, saves):
        load.wait()
        save.start()
    for save in saves:
        save.wait()


def on_device(tokens, left_factor, right_factor, gate_kernel, out_grad):
    hbm = pl.BlockSpec(memory_space=pl.ANY)
    plane = pltpu.VMEM((S2, D), BF16)
    square = pltpu.VMEM((S2, S2), BF16)
    tile, four = pltpu.VMEM((8, S1), F32), pltpu.VMEM((4, S1), F32)
    half = S2 // 2
    dma = pltpu.SemaphoreType.DMA
    results = (
        jax.ShapeDtypeStruct((S2, D), BF16),
        jax.ShapeDtypeStruct((S2, D), BF16),
        jax.ShapeDtypeStruct((S2, S2), F32),
        jax.ShapeDtypeStruct((S1, S1), F32),
        jax.ShapeDtypeStruct((4, S1), F32),
    )
    made = pl.pallas_call(
        kernel,
        name="monarch",
        out_shape=results,
        in_specs=[hbm] * 5,
        out_specs=(hbm,) * 5,
        scratch_shapes=[
            plane, square, pltpu.VMEM((S1, S1), BF16),
            *[plane] * 12,
            pltpu.VMEM((S2, D), F32),
            *[plane] * 4,
            square, square, pltpu.VMEM((S2, S1), BF16), square, square,
            four, pltpu.VMEM((S2, S1), F32), pltpu.VMEM((S2, S1), F32),
            *[pltpu.VMEM((half, S2), F32)] * 3,
            pltpu.VMEM((NC - 1, half // NC, S2), F32),
            pltpu.VMEM((8, 8, S1), F32), pltpu.VMEM((NZ, 8, S1), F32), tile,
            pltpu.VMEM((S2, S2), F32), pltpu.VMEM((S2, S2), F32), pltpu.VMEM((S1, S1), F32),
            pltpu.VMEM((NC - 1, 8, S1), F32), tile, tile, tile, pltpu.VMEM((NZ, 8, S1), F32), tile,
            pltpu.VMEM((S1, S1), F32),
            *[four] * 6,
            dma((3,)), dma((17,)), dma((4,)), dma((4,)), dma((4,)), dma((4,)),
            dma((13,)), dma((13,)), dma((2,)), dma((NC - 1,)),
        ],
        compiler_params=pltpu.CompilerParams(
            collective_id=0, has_side_effects=True, vmem_limit_bytes=VMEM_LIMIT
        ),
    )(tokens.reshape(S2, D), left_factor, right_factor, gate_kernel.T, out_grad.reshape(S2, D))
    mixed, tgrad, lgrad, rgrad, kgrad = pl.pallas_call(
        keep,
        name="keep",
        out_shape=results,
        in_specs=[hbm] * 5,
        out_specs=(hbm,) * 5,
        scratch_shapes=[
            *[pltpu.VMEM(result.shape, result.dtype) for result in results],
            dma((3 * KEEP_PARTS + 2,)), dma((3 * KEEP_PARTS + 2,)),
        ],
    )(*made)
    return mixed.reshape(tokens.shape), tgrad.reshape(tokens.shape), lgrad, rgrad, kgrad.T


def solution(mesh):
    blocks = P("dp", "seq", None, None)
    return jax.shard_map(
        on_device,
        mesh=mesh,
        in_specs=(blocks, P(), P(), P(None, "seq"), blocks),
        out_specs=(blocks, blocks, P(), P(), P(None, "seq")),
        check_vma=False,
    )
```

```python
import math

import jax
import jax.numpy as jnp
from jax import lax
from jax.experimental import pallas as pl
from jax.experimental.pallas import tpu as pltpu
from jax.sharding import PartitionSpec as P

MESH = pl.DeviceIdType.MESH
BF16, F32 = jnp.bfloat16, jnp.float32
D, S2, S1, BATCH = 768, 512, 128, 4
NZ, NQ, NC = 16, 8, 16
ZROWS, QROWS = S2 // NZ, S2 // NQ
LANES = 256
ZORDER = [8, -7, 7, -6, 6, -5, 5, -4, 4, -3, 3, -2, 2, -1, 1]
MPARTS = [[8, -7, 7, -1, 1], [-6, 6, -4, 4, -3, 3], [-5, 5, -2, 2]]
LASTPARTS = [[8, -7, 7], [-6, 6, -5, 5, -4, 4, -3, 3, -2, 2, -1, 1]]
LPARTS = [(0, 512), (512, 256)]
KEEP_PARTS = 4
VMEM_LIMIT = 56 * 1024 * 1024
LEFT_SCALE = 1.0 / math.sqrt(BATCH * S1 * D)
RIGHT_SCALE = 1.0 / math.sqrt(BATCH * S2 * D)
KERNEL_SCALE = 1.0 / math.sqrt(BATCH * D)


def dot(a, b, dims=((1,), (0,)), precision=None):
    return lax.dot_general(a, b, (dims, ((), ())), preferred_element_type=F32, precision=precision)


def iotas(rows, columns):
    return (
        lax.broadcasted_iota(jnp.int32, (rows, columns), 0),
        lax.broadcasted_iota(jnp.int32, (rows, columns), 1),
    )


def lane_tiles(body, part=(0, D)):
    def step(t, carry):
        body(pl.ds(pl.multiple_of(t * LANES, LANES), LANES))
        return carry

    lax.fori_loop(part[0] // LANES, (part[0] + part[1]) // LANES, step, 0)


def kernel(
    tokens_hbm, left_hbm, right_hbm, gate_hbm, grad_hbm,
    mixed_ref, tgrad_ref, lgrad_ref, rgrad_ref, kgrad_ref,
    tokens, left_ref, right_ref, first, g1, g1p, g2, weighted, bo, b1, b1p, b2, f1, f1p, f2, blended, mo, m1, m1p, tgrad,
    to_q, to_z, expand, mix, mix_t, gate_mine, gate_col, ksum,
    left_give, left_mate, left_half, left_xy, z_send, z_recv, piece,
    lgrad, pairs, right_local, right_xy, right_sum, right_mate, right_half, right_z, right_piece, rgrad,
    k_local, k_core, k_half, k_hi, k_total, k_home,
    load_sem, own_sem, z_ss, z_rs, q_ss, q_rs, s_ss, s_rs, x_ss, x_rs,
):
    dp, me = lax.axis_index("dp"), lax.axis_index("seq")
    z, q = lax.rem(me, NZ), lax.div(me, NZ)
    core, x_hi = lax.rem(dp, 2), lax.div(dp, 2)
    chip = x_hi * NQ + q
    mate = (x_hi * 2 + (1 - core), me)
    across = ((1 - x_hi) * 2 + core, me)
    z_peers = [lax.rem(z + d + NZ, NZ) for d in ZORDER]
    q_peers = [lax.bitwise_xor(q, d) for d in range(1, NQ)]
    chip_peers = [lax.bitwise_xor(chip, d) for d in range(1, NC)]

    def along_z(zz):
        return (dp, q * NZ + zz)

    def along_q(qq):
        return (dp, qq * NZ + z)

    def at_chip(cc):
        return (lax.div(cc, NQ) * 2 + core, lax.rem(cc, NQ) * NZ + z)

    user = lax.rem(me, NQ) * NZ + lax.div(me, NQ)
    holder = z * NQ + q
    moves = user != me

    barrier = pltpu.get_barrier_semaphore()

    def greet(device):
        pl.semaphore_signal(barrier, inc=1, device_id=device, device_id_type=MESH)

    for zz in z_peers:
        greet(along_z(zz))

    @pl.when(moves)
    def _():
        greet((dp, user))
        greet((dp, holder))

    for cc in chip_peers:
        greet(at_chip(cc))
    greet(mate)
    loads = [
        pltpu.make_async_copy(src, dst, load_sem.at[n])
        for n, (src, dst) in enumerate([(tokens_hbm, tokens), (left_hbm, left_ref), (right_hbm, right_ref)])
    ]
    for load in loads:
        load.start()
    pl.semaphore_wait(barrier, jnp.where(moves, NZ + NC + 1, NZ + NC - 1))

    def send(src, dst, ss, rs, device):
        copy = pltpu.make_async_remote_copy(
            src_ref=src, dst_ref=dst, send_sem=ss, recv_sem=rs, device_id=device, device_id_type=MESH
        )
        copy.start()
        return copy

    def block(ref, index, rows, lanes=None):
        spot = pl.ds(pl.multiple_of(index * rows, rows), rows)
        return ref.at[spot] if lanes is None else ref.at[spot, pl.ds(*lanes)]

    def z_part(n, p, src, dst, distances):
        for d in distances:
            zz = z_peers[ZORDER.index(d)]
            send(
                block(src, zz, ZROWS, LPARTS[p]), block(dst, z, ZROWS, LPARTS[p]),
                z_ss.at[2 * n + p], z_rs.at[2 * n + p], along_z(zz),
            )

    def z_own(n, p, src, dst):
        own = pltpu.make_async_copy(
            block(src, z, ZROWS, LPARTS[p]), block(dst, z, ZROWS, LPARTS[p]), own_sem.at[2 * n + p]
        )
        own.start()
        return own

    def q_exchange(n, p, src, dst):
        own = pltpu.make_async_copy(
            block(src, q, QROWS, LPARTS[p]), block(dst, q, QROWS, LPARTS[p]), own_sem.at[8 + 2 * n + p]
        )
        own.start()
        for qq in q_peers:
            send(
                block(src, qq, QROWS, LPARTS[p]), block(dst, q, QROWS, LPARTS[p]),
                q_ss.at[2 * n + p], q_rs.at[2 * n + p], along_q(qq),
            )
        return own

    def bytes_of(ref, sem):
        pltpu.make_async_copy(ref, ref, sem).wait()

    def z_bytes(p, ref, sem):
        bytes_of(ref.at[pl.ds(0, S2 - ZROWS), pl.ds(*LPARTS[p])], sem)

    def q_bytes(p, ref, sem):
        bytes_of(ref.at[pl.ds(0, S2 - QROWS), pl.ds(*LPARTS[p])], sem)

    def z_arrive(n, p, own, dst):
        own.wait()
        z_bytes(p, dst, z_rs.at[2 * n + p])

    def q_arrive(n, p, own, dst):
        own.wait()
        q_bytes(p, dst, q_rs.at[2 * n + p])

    def move(src, dst, n, device):
        remote = pltpu.make_async_remote_copy(
            src_ref=src, dst_ref=dst, send_sem=s_ss.at[n], recv_sem=s_rs.at[n], device_id=device, device_id_type=MESH
        )
        local = pltpu.make_async_copy(src, dst, own_sem.at[16 + n])

        @pl.when(moves)
        def _():
            remote.start()

        @pl.when(jnp.logical_not(moves))
        def _():
            local.start()

        def finish():
            @pl.when(moves)
            def _():
                remote.wait()

            @pl.when(jnp.logical_not(moves))
            def _():
                local.wait()

        return finish

    gate_moved = move(gate_hbm, gate_mine, 0, (dp, user))
    z_part(0, 0, grad_hbm, g1, ZORDER)
    z_part(0, 1, grad_hbm, g1, ZORDER)
    g_own = [z_own(0, p, grad_hbm, g1) for p in (0, 1)]

    loads[0].wait()
    loads[1].wait()

    def step_first(lanes):
        first[:, lanes] = dot(left_ref[...], tokens[:, lanes]).astype(BF16)

    lane_tiles(step_first)

    r, c = iotas(S2, S2)
    to_q[...] = jnp.where((r // 4 % NZ) * ZROWS + (r // QROWS) * 4 + r % 4 == c, 1.0, 0.0).astype(BF16)
    to_z[...] = jnp.where((c // 4 % NZ) * ZROWS + (c // QROWS) * 4 + c % 4 == r, 1.0, 0.0).astype(BF16)
    re, ce = iotas(S2, S1)
    expand[...] = jnp.where(re // 4 == ce, 1.0, 0.0).astype(BF16)
    same = (r % 4 == c % 4).astype(F32)
    loads[2].wait()
    wide = dot(expand[...], right_ref[...]).astype(BF16)
    mix[...] = (dot(wide, expand[...], ((1,), (1,))) * same).astype(BF16)
    wide_t = dot(expand[...], right_ref[...], ((1,), (1,))).astype(BF16)
    mix_t[...] = (dot(wide_t, expand[...], ((1,), (1,))) * same).astype(BF16)
    gate_moved()
    pick = jnp.where(re % 4 == ce, 1.0, 0.0)
    gates = jnp.concatenate([gate_mine[...], jnp.zeros((S1 - 4, S1), F32)], axis=0)
    spread = dot(expand[...].astype(F32), gates, ((1,), (1,)), lax.Precision.HIGHEST)
    gate_col[...] = jnp.broadcast_to(jnp.sum(spread * pick, axis=1, keepdims=True), (S2, S1))

    def reorder(matrix, p, src, dst):
        def step(lanes):
            dst[:, lanes] = dot(matrix[...], src[:, lanes]).astype(BF16)

        lane_tiles(step, LPARTS[p])

    def step_back(lanes):
        w = (gate_col[:, 0:1] * g2[:, lanes].astype(F32)).astype(BF16)
        weighted[:, lanes] = w
        bo[:, lanes] = dot(mix_t[...], w).astype(BF16)

    def step_mixed(lanes):
        value = dot(mix[...], f2[:, lanes])
        blended[:, lanes] = value
        mo[:, lanes] = (gate_col[:, 0:1] * value).astype(BF16)

    ksum[...] = jnp.zeros((S2, S1), F32)
    pairs[...] = jnp.zeros((S2, S2), F32)

    def step_kernel(lanes):
        rows = jnp.sum(g2[:, lanes].astype(F32) * blended[:, lanes], axis=1, keepdims=True)
        ksum[...] += jnp.broadcast_to(rows, (S2, S1))

    def step_right(lanes):
        pairs[...] += dot(weighted[:, lanes], f2[:, lanes], ((1,), (1,)))

    z_bytes(0, g1, z_ss.at[0])
    f_own = [z_own(1, p, first, f1) for p in (0, 1)]
    z_part(1, 0, first, f1, ZORDER)

    z_arrive(0, 0, g_own[0], g1)
    reorder(to_q, 0, g1, g1p)
    q_arrive(0, 0, q_exchange(0, 0, g1p, g2), g2)
    lane_tiles(step_back, LPARTS[0])
    bq0 = q_exchange(1, 0, bo, b1)
    z_arrive(0, 1, g_own[1], g1)
    reorder(to_q, 1, g1, g1p)
    gq1 = q_exchange(0, 1, g1p, g2)
    q_arrive(1, 0, bq0, b1)
    reorder(to_z, 0, b1, b1p)
    z_part(2, 0, b1p, b2, ZORDER)
    q_arrive(0, 1, gq1, g2)
    lane_tiles(step_back, LPARTS[1])
    q_arrive(1, 1, q_exchange(1, 1, bo, b1), b1)
    reorder(to_z, 1, b1, b1p)
    z_part(2, 1, b1p, b2, ZORDER)
    b_own = [z_own(2, p, b1p, b2) for p in (0, 1)]

    z_arrive(1, 0, f_own[0], f1)
    reorder(to_q, 0, f1, f1p)
    q_arrive(2, 0, q_exchange(2, 0, f1p, f2), f2)
    lane_tiles(step_mixed, LPARTS[0])
    mq0 = q_exchange(3, 0, mo, m1)
    lane_tiles(step_kernel, LPARTS[0])
    lane_tiles(step_right, LPARTS[0])
    q_arrive(3, 0, mq0, m1)
    reorder(to_z, 0, m1, m1p)
    z_bytes(0, b2, z_ss.at[4])
    z_part(1, 1, first, f1, ZORDER)

    half = S2 // 2
    rows_l = half // NC

    def left_rows(index, p):
        spot = pl.ds(pl.multiple_of(index * half, half), half)
        lanes = pl.ds(*LPARTS[p])
        return dot(b2[spot, lanes], tokens[:, lanes], ((1,), (1,)))

    z_arrive(2, 0, b_own[0], b2)
    left_give[...] = left_rows(1 - core, 0)
    left_half[...] = left_rows(core, 0)
    m_own = [z_own(3, 0, m1p, mixed_ref)]
    z_arrive(2, 1, b_own[1], b2)
    left_give[...] += left_rows(1 - core, 1)
    c1 = send(left_give, left_mate, s_ss.at[5], s_rs.at[5], mate)
    z_part(3, 0, m1p, mixed_ref, MPARTS[0])
    left_half[...] += left_rows(core, 1)
    c1.wait()
    left_half[...] += left_mate[...]
    for j, cc in enumerate(chip_peers):
        send(block(left_half, cc, rows_l), left_xy.at[j], s_ss.at[8], s_rs.at[8], at_chip(cc))

    def step_tokens(lanes):
        tgrad[:, lanes] = dot(left_ref[...], b2[:, lanes], ((0,), (0,))).astype(BF16)

    lane_tiles(step_tokens)
    save_tokens = pltpu.make_async_copy(tgrad, tgrad_ref, own_sem.at[20])
    save_tokens.start()

    z_arrive(1, 1, f_own[1], f1)
    reorder(to_q, 1, f1, f1p)
    fq1 = q_exchange(2, 1, f1p, f2)

    sum_l = left_half[pl.ds(pl.multiple_of(chip * rows_l, rows_l), rows_l), :]
    bytes_of(left_xy, s_ss.at[8])
    bytes_of(left_xy, s_rs.at[8])
    for j in range(NC - 1):
        sum_l = sum_l + left_xy[j]
    for n in range(8):
        z_send[n] = sum_l[n // 4 * 8 : n // 4 * 8 + 8, n % 4 * 128 : n % 4 * 128 + 128]
    z_recv[z] = z_send[lax.rem(z, 8)]
    for zz in z_peers:
        send(z_send.at[lax.rem(zz, 8)], z_recv.at[z], s_ss.at[9], s_rs.at[9], along_z(zz))
    z_part(3, 0, m1p, mixed_ref, MPARTS[1])

    q_arrive(2, 1, fq1, f2)
    lane_tiles(step_mixed, LPARTS[1])
    mq1 = q_exchange(3, 1, mo, m1)

    lane_tiles(step_kernel, LPARTS[1])
    by_block = dot(expand[...].astype(F32), ksum[...] * pick, ((0,), (0,)), lax.Precision.HIGHEST)
    k_local[...] = by_block.T[0:4, :]
    k1 = send(k_local, k_core, s_ss.at[1], s_rs.at[1], mate)

    lane_tiles(step_right, LPARTS[1])
    halves = dot(expand[...].astype(F32), pairs[...] * same, ((0,), (0,)), lax.Precision.HIGHEST)
    right_local[...] = dot(halves, expand[...].astype(F32), ((1,), (0,)), lax.Precision.HIGHEST)
    for j, cc in enumerate(chip_peers):
        send(block(right_local, cc, 8), right_xy.at[j], s_ss.at[6], s_rs.at[6], at_chip(cc))
    k1.wait()
    k_half[...] = k_local[...] + k_core[...]
    k2 = send(k_half, k_hi, s_ss.at[2], s_rs.at[2], across)

    z_tiles = right_z.at[pl.ds(0, NZ - 1)]
    bytes_of(z_tiles, s_ss.at[9])
    bytes_of(z_tiles, s_rs.at[9])
    whole_l = z_recv[0]
    for n in range(1, NZ):
        whole_l = whole_l + z_recv[n]
    piece[...] = whole_l * LEFT_SCALE
    first_row = core * half + chip * rows_l
    part = lax.rem(z, 8)
    spot_l = lgrad.at[
        pl.ds(pl.multiple_of(first_row + part // 4 * 8, 8), 8), pl.ds(pl.multiple_of(part % 4 * 128, 128), 128)
    ]
    own_l = pltpu.make_async_copy(piece, spot_l, own_sem.at[21])
    own_l.start()
    for d in (-4, 3, -3, 2, -2, 1, -1):
        zz = z_peers[ZORDER.index(d)]
        send(piece, spot_l, s_ss.at[11], s_rs.at[11], along_z(zz))
    sum_r = right_local[pl.ds(pl.multiple_of(chip * 8, 8), 8), :]
    bytes_of(right_xy, s_ss.at[6])
    bytes_of(right_xy, s_rs.at[6])
    for j in range(NC - 1):
        sum_r = sum_r + right_xy[j]
    right_half[...] = sum_r
    right_z[z] = sum_r
    for zz in z_peers:
        send(right_half, right_z.at[z], s_ss.at[7], s_rs.at[7], along_z(zz))
    z_part(3, 0, m1p, mixed_ref, MPARTS[2])

    q_arrive(3, 1, mq1, m1)
    reorder(to_z, 1, m1, m1p)
    m_own.append(z_own(3, 1, m1p, mixed_ref))
    z_part(3, 1, m1p, mixed_ref, LASTPARTS[0])
    k2.wait()
    k_total[...] = (k_half[...] + k_hi[...]) * KERNEL_SCALE
    kernel_moved = move(k_total, k_home, 3, (dp, holder))
    z_part(3, 1, m1p, mixed_ref, LASTPARTS[1])

    own_l.wait()
    seven = z_recv.at[pl.ds(0, 7)]
    bytes_of(seven, s_ss.at[11])
    bytes_of(seven, s_rs.at[11])

    def part_l(which, cc):
        return lgrad.at[pl.ds(pl.multiple_of(which * half + cc * rows_l, rows_l), rows_l)]

    mine = part_l(core, chip)
    lx = [send(mine, mine, x_ss.at[0], x_rs.at[j], at_chip(cc)) for j, cc in enumerate(chip_peers)]
    send(mine, mine, x_ss.at[1], s_rs.at[12], mate)

    bytes_of(z_tiles, s_ss.at[7])
    bytes_of(z_tiles, s_rs.at[7])
    whole_r = right_z[0]
    for n in range(1, NZ):
        whole_r = whole_r + right_z[n]
    right_sum[...] = whole_r
    rm = send(right_sum, right_mate, s_ss.at[4], s_rs.at[4], mate)
    rm.wait()
    right_piece[...] = (right_sum[...] + right_mate[...]) * RIGHT_SCALE
    rgrad[pl.ds(pl.multiple_of(chip * 8, 8), 8), :] = right_piece[...]
    for cc in chip_peers:
        send(right_piece, block(rgrad, chip, 8), s_ss.at[10], s_rs.at[10], at_chip(cc))
    for j, cc in enumerate(chip_peers):
        lx[j].wait_recv()
        send(part_l(core, cc), part_l(core, cc), x_ss.at[1], s_rs.at[12], mate)
    bytes_of(left_xy, x_ss.at[0])
    bytes_of(lgrad.at[pl.ds(0, half)], x_ss.at[1])
    bytes_of(lgrad.at[pl.ds(0, half)], s_rs.at[12])
    save_left = pltpu.make_async_copy(lgrad, lgrad_ref, own_sem.at[24])
    save_left.start()
    kernel_moved()
    bytes_of(right_xy, s_ss.at[10])
    bytes_of(right_xy, s_rs.at[10])
    saves = [
        pltpu.make_async_copy(src, dst, own_sem.at[22 + n])
        for n, (src, dst) in enumerate([(k_home, kgrad_ref), (rgrad, rgrad_ref)])
    ]
    for save in saves:
        save.start()
    save_tokens.wait()
    save_left.wait()
    for n, p, buffer in [(0, 1, g1), (1, 0, f1), (1, 1, f1), (2, 1, b2), (3, 0, m1p), (3, 1, m1p)]:
        z_bytes(p, buffer, z_ss.at[2 * n + p])
    for n, buffer in enumerate([g2, b1, f2, m1]):
        for p in (0, 1):
            q_bytes(p, buffer, q_ss.at[2 * n + p])
    for p in (0, 1):
        m_own[p].wait()
        z_bytes(p, m1p, z_rs.at[6 + p])
    for save in saves:
        save.wait()


def keep(*refs):
    pieces = []
    for n in range(5):
        rows = refs[n].shape[0]
        step = max(rows // KEEP_PARTS, 4) if rows == S2 else rows
        pieces += [(n, at, step) for at in range(0, rows, step)]
    load_sem, save_sem = refs[15], refs[16]
    loads, saves = [], []
    for i, (n, at, step) in enumerate(pieces):
        spot = pl.ds(at, step)
        loads.append(pltpu.make_async_copy(refs[n].at[spot], refs[10 + n].at[spot], load_sem.at[i]))
        saves.append(pltpu.make_async_copy(refs[10 + n].at[spot], refs[5 + n].at[spot], save_sem.at[i]))
        loads[-1].start()
    for load, save in zip(loads, saves):
        load.wait()
        save.start()
    for save in saves:
        save.wait()


def on_device(tokens, left_factor, right_factor, gate_kernel, out_grad):
    hbm = pl.BlockSpec(memory_space=pl.ANY)
    plane = pltpu.VMEM((S2, D), BF16)
    square = pltpu.VMEM((S2, S2), BF16)
    tile, four = pltpu.VMEM((8, S1), F32), pltpu.VMEM((4, S1), F32)
    half = S2 // 2
    dma = pltpu.SemaphoreType.DMA
    results = (
        jax.ShapeDtypeStruct((S2, D), BF16),
        jax.ShapeDtypeStruct((S2, D), BF16),
        jax.ShapeDtypeStruct((S2, S2), F32),
        jax.ShapeDtypeStruct((S1, S1), F32),
        jax.ShapeDtypeStruct((4, S1), F32),
    )
    made = pl.pallas_call(
        kernel,
        name="monarch",
        out_shape=results,
        in_specs=[hbm] * 5,
        out_specs=(hbm,) * 5,
        scratch_shapes=[
            plane, square, pltpu.VMEM((S1, S1), BF16),
            *[plane] * 12,
            pltpu.VMEM((S2, D), F32),
            *[plane] * 4,
            square, square, pltpu.VMEM((S2, S1), BF16), square, square,
            four, pltpu.VMEM((S2, S1), F32), pltpu.VMEM((S2, S1), F32),
            *[pltpu.VMEM((half, S2), F32)] * 3,
            pltpu.VMEM((NC - 1, half // NC, S2), F32),
            pltpu.VMEM((8, 8, S1), F32), pltpu.VMEM((NZ, 8, S1), F32), tile,
            pltpu.VMEM((S2, S2), F32), pltpu.VMEM((S2, S2), F32), pltpu.VMEM((S1, S1), F32),
            pltpu.VMEM((NC - 1, 8, S1), F32), tile, tile, tile, pltpu.VMEM((NZ, 8, S1), F32), tile,
            pltpu.VMEM((S1, S1), F32),
            *[four] * 6,
            dma((3,)), dma((25,)), dma((8,)), dma((8,)), dma((8,)), dma((8,)),
            dma((13,)), dma((13,)), dma((2,)), dma((NC - 1,)),
        ],
        compiler_params=pltpu.CompilerParams(
            collective_id=0, has_side_effects=True, vmem_limit_bytes=VMEM_LIMIT
        ),
    )(tokens.reshape(S2, D), left_factor, right_factor, gate_kernel.T, out_grad.reshape(S2, D))
    mixed, tgrad, lgrad, rgrad, kgrad = pl.pallas_call(
        keep,
        name="keep",
        out_shape=results,
        in_specs=[hbm] * 5,
        out_specs=(hbm,) * 5,
        scratch_shapes=[
            *[pltpu.VMEM(result.shape, result.dtype) for result in results],
            dma((3 * KEEP_PARTS + 2,)), dma((3 * KEEP_PARTS + 2,)),
        ],
    )(*made)
    return mixed.reshape(tokens.shape), tgrad.reshape(tokens.shape), lgrad, rgrad, kgrad.T


def solution(mesh):
    blocks = P("dp", "seq", None, None)
    return jax.shard_map(
        on_device,
        mesh=mesh,
        in_specs=(blocks, P(), P(), P(None, "seq"), blocks),
        out_specs=(blocks, blocks, P(), P(), P(None, "seq")),
        check_vma=False,
    )
```

```python
import math

import jax
import jax.numpy as jnp
from jax import lax
from jax.experimental import pallas as pl
from jax.experimental.pallas import tpu as pltpu
from jax.sharding import PartitionSpec as P

MESH = pl.DeviceIdType.MESH
BF16, F32 = jnp.bfloat16, jnp.float32
D, S2, S1, BATCH = 768, 512, 128, 4
NZ, NQ, NC = 16, 8, 16
ZROWS, QROWS = S2 // NZ, S2 // NQ
LANES = 256
ZORDER = [8, -7, 7, -6, 6, -5, 5, -4, 4, -3, 3, -2, 2, -1, 1]
MPARTS = [[8, -7, 7, -1, 1], [-6, 6, -4, 4, -3, 3], [-5, 5, -2, 2]]
LASTPARTS = [[8, -7, 7], [-6, 6, -5, 5, -4, 4, -3, 3, -2, 2, -1, 1]]
LPARTS = [(0, 512), (512, 256)]
KEEP_PARTS = 4
VMEM_LIMIT = 56 * 1024 * 1024
LEFT_SCALE = 1.0 / math.sqrt(BATCH * S1 * D)
RIGHT_SCALE = 1.0 / math.sqrt(BATCH * S2 * D)
KERNEL_SCALE = 1.0 / math.sqrt(BATCH * D)


def dot(a, b, dims=((1,), (0,)), precision=None):
    return lax.dot_general(a, b, (dims, ((), ())), preferred_element_type=F32, precision=precision)


def iotas(rows, columns):
    return (
        lax.broadcasted_iota(jnp.int32, (rows, columns), 0),
        lax.broadcasted_iota(jnp.int32, (rows, columns), 1),
    )


def lane_tiles(body, part=(0, D)):
    def step(t, carry):
        body(pl.ds(pl.multiple_of(t * LANES, LANES), LANES))
        return carry

    lax.fori_loop(part[0] // LANES, (part[0] + part[1]) // LANES, step, 0)


def kernel(
    tokens_hbm, left_hbm, right_hbm, gate_hbm, grad_hbm,
    mixed_ref, tgrad_ref, lgrad_ref, rgrad_ref, kgrad_ref,
    grad, tokens, left_ref, right_ref, first, g1, g1p, g2, weighted, bo, b1, b1p, b2, f1, f1p, f2, blended, mo, m1, m1p, tgrad,
    to_q, to_z, expand, mix, mix_t, gate_mine, gate_col, ksum,
    left_give, left_mate, left_half, left_xy, z_send, z_recv, piece, z_gather, own_rows,
    lgrad, pairs, right_local, right_xy, right_half, right_z, right_piece, right_all, rgrad,
    k_local, k_core, k_half, k_hi, k_total, k_home,
    load_sem, own_sem, z_ss, z_rs, q_ss, q_rs, s_ss, s_rs, x_ss, x_rs,
):
    dp, me = lax.axis_index("dp"), lax.axis_index("seq")
    z, q = lax.rem(me, NZ), lax.div(me, NZ)
    core, x_hi = lax.rem(dp, 2), lax.div(dp, 2)
    chip = x_hi * NQ + q
    mate = (x_hi * 2 + (1 - core), me)
    across = ((1 - x_hi) * 2 + core, me)
    z_peers = [lax.rem(z + d + NZ, NZ) for d in ZORDER]
    q_peers = [lax.bitwise_xor(q, d) for d in range(1, NQ)]
    chip_peers = [lax.bitwise_xor(chip, d) for d in range(1, NC)]

    def along_z(zz):
        return (dp, q * NZ + zz)

    def along_q(qq):
        return (dp, qq * NZ + z)

    def at_chip(cc, on=core):
        return (lax.div(cc, NQ) * 2 + on, lax.rem(cc, NQ) * NZ + z)

    plane_peers = [(at_chip(cc), core * NC + cc) for cc in chip_peers]
    for d in range(NC):
        cc = lax.bitwise_xor(chip, d)
        plane_peers.append((at_chip(cc, 1 - core), (1 - core) * NC + cc))
    number = core * NC + chip

    user = lax.rem(me, NQ) * NZ + lax.div(me, NQ)
    holder = z * NQ + q
    moves = user != me

    loads = [
        pltpu.make_async_copy(src, dst, load_sem.at[n])
        for n, (src, dst) in enumerate(
            [(grad_hbm, grad), (tokens_hbm, tokens), (left_hbm, left_ref), (right_hbm, right_ref)]
        )
    ]
    for load in loads:
        load.start()
    barrier = pltpu.get_barrier_semaphore()

    def greet(device):
        pl.semaphore_signal(barrier, inc=1, device_id=device, device_id_type=MESH)

    for zz in z_peers:
        greet(along_z(zz))

    @pl.when(moves)
    def _():
        greet((dp, user))
        greet((dp, holder))

    for cc in chip_peers:
        greet(at_chip(cc))
    for d in range(NC):
        greet(at_chip(lax.bitwise_xor(chip, d), 1 - core))
    pl.semaphore_wait(barrier, jnp.where(moves, NZ + 2 * NC, NZ + 2 * NC - 2))

    def send(src, dst, ss, rs, device):
        copy = pltpu.make_async_remote_copy(
            src_ref=src, dst_ref=dst, send_sem=ss, recv_sem=rs, device_id=device, device_id_type=MESH
        )
        copy.start()
        return copy

    def block(ref, index, rows, lanes=None):
        spot = pl.ds(pl.multiple_of(index * rows, rows), rows)
        return ref.at[spot] if lanes is None else ref.at[spot, pl.ds(*lanes)]

    def z_part(n, p, src, dst, distances):
        for d in distances:
            zz = z_peers[ZORDER.index(d)]
            send(
                block(src, zz, ZROWS, LPARTS[p]), block(dst, z, ZROWS, LPARTS[p]),
                z_ss.at[2 * n + p], z_rs.at[2 * n + p], along_z(zz),
            )

    def z_own(n, p, src, dst):
        own = pltpu.make_async_copy(
            block(src, z, ZROWS, LPARTS[p]), block(dst, z, ZROWS, LPARTS[p]), own_sem.at[2 * n + p]
        )
        own.start()
        return own

    def q_exchange(n, p, src, dst):
        own = pltpu.make_async_copy(
            block(src, q, QROWS, LPARTS[p]), block(dst, q, QROWS, LPARTS[p]), own_sem.at[8 + 2 * n + p]
        )
        own.start()
        for qq in q_peers:
            send(
                block(src, qq, QROWS, LPARTS[p]), block(dst, q, QROWS, LPARTS[p]),
                q_ss.at[2 * n + p], q_rs.at[2 * n + p], along_q(qq),
            )
        return own

    def bytes_of(ref, sem):
        pltpu.make_async_copy(ref, ref, sem).wait()

    def z_bytes(p, ref, sem):
        bytes_of(ref.at[pl.ds(0, S2 - ZROWS), pl.ds(*LPARTS[p])], sem)

    def q_bytes(p, ref, sem):
        bytes_of(ref.at[pl.ds(0, S2 - QROWS), pl.ds(*LPARTS[p])], sem)

    def z_arrive(n, p, own, dst):
        own.wait()
        z_bytes(p, dst, z_rs.at[2 * n + p])

    def q_arrive(n, p, own, dst):
        own.wait()
        q_bytes(p, dst, q_rs.at[2 * n + p])

    def move(src, dst, n, device):
        remote = pltpu.make_async_remote_copy(
            src_ref=src, dst_ref=dst, send_sem=s_ss.at[n], recv_sem=s_rs.at[n], device_id=device, device_id_type=MESH
        )
        local = pltpu.make_async_copy(src, dst, own_sem.at[16 + n])

        @pl.when(moves)
        def _():
            remote.start()

        @pl.when(jnp.logical_not(moves))
        def _():
            local.start()

        def finish():
            @pl.when(moves)
            def _():
                remote.wait()

            @pl.when(jnp.logical_not(moves))
            def _():
                local.wait()

        return finish

    gate_moved = move(gate_hbm, gate_mine, 0, (dp, user))
    loads[0].wait()
    z_part(0, 0, grad, g1, ZORDER)
    z_part(0, 1, grad, g1, ZORDER)
    g_own = [z_own(0, p, grad, g1) for p in (0, 1)]

    loads[1].wait()
    loads[2].wait()

    def step_first(lanes):
        first[:, lanes] = dot(left_ref[...], tokens[:, lanes]).astype(BF16)

    lane_tiles(step_first)

    r, c = iotas(S2, S2)
    to_q[...] = jnp.where((r // 4 % NZ) * ZROWS + (r // QROWS) * 4 + r % 4 == c, 1.0, 0.0).astype(BF16)
    to_z[...] = jnp.where((c // 4 % NZ) * ZROWS + (c // QROWS) * 4 + c % 4 == r, 1.0, 0.0).astype(BF16)
    re, ce = iotas(S2, S1)
    expand[...] = jnp.where(re // 4 == ce, 1.0, 0.0).astype(BF16)
    same = (r % 4 == c % 4).astype(F32)
    loads[3].wait()
    wide = dot(expand[...], right_ref[...]).astype(BF16)
    mix[...] = (dot(wide, expand[...], ((1,), (1,))) * same).astype(BF16)
    wide_t = dot(expand[...], right_ref[...], ((1,), (1,))).astype(BF16)
    mix_t[...] = (dot(wide_t, expand[...], ((1,), (1,))) * same).astype(BF16)
    gate_moved()
    pick = jnp.where(re % 4 == ce, 1.0, 0.0)
    gates = jnp.concatenate([gate_mine[...], jnp.zeros((S1 - 4, S1), F32)], axis=0)
    spread = dot(expand[...].astype(F32), gates, ((1,), (1,)), lax.Precision.HIGHEST)
    gate_col[...] = jnp.broadcast_to(jnp.sum(spread * pick, axis=1, keepdims=True), (S2, S1))

    def reorder(matrix, p, src, dst):
        def step(lanes):
            dst[:, lanes] = dot(matrix[...], src[:, lanes]).astype(BF16)

        lane_tiles(step, LPARTS[p])

    def step_back(lanes):
        w = (gate_col[:, 0:1] * g2[:, lanes].astype(F32)).astype(BF16)
        weighted[:, lanes] = w
        bo[:, lanes] = dot(mix_t[...], w).astype(BF16)

    def step_mixed(lanes):
        value = dot(mix[...], f2[:, lanes])
        blended[:, lanes] = value
        mo[:, lanes] = (gate_col[:, 0:1] * value).astype(BF16)

    ksum[...] = jnp.zeros((S2, S1), F32)
    pairs[...] = jnp.zeros((S2, S2), F32)

    def step_kernel(lanes):
        rows = jnp.sum(g2[:, lanes].astype(F32) * blended[:, lanes], axis=1, keepdims=True)
        ksum[...] += jnp.broadcast_to(rows, (S2, S1))

    def step_right(lanes):
        pairs[...] += dot(weighted[:, lanes], f2[:, lanes], ((1,), (1,)))

    z_bytes(0, g1, z_ss.at[0])
    f_own = [z_own(1, p, first, f1) for p in (0, 1)]
    z_part(1, 0, first, f1, ZORDER)

    z_arrive(0, 0, g_own[0], g1)
    reorder(to_q, 0, g1, g1p)
    q_arrive(0, 0, q_exchange(0, 0, g1p, g2), g2)
    lane_tiles(step_back, LPARTS[0])
    bq0 = q_exchange(1, 0, bo, b1)
    z_arrive(0, 1, g_own[1], g1)
    reorder(to_q, 1, g1, g1p)
    gq1 = q_exchange(0, 1, g1p, g2)
    q_arrive(1, 0, bq0, b1)
    reorder(to_z, 0, b1, b1p)
    z_part(2, 0, b1p, b2, ZORDER)
    q_arrive(0, 1, gq1, g2)
    lane_tiles(step_back, LPARTS[1])
    q_arrive(1, 1, q_exchange(1, 1, bo, b1), b1)
    reorder(to_z, 1, b1, b1p)
    z_part(2, 1, b1p, b2, ZORDER)
    b_own = [z_own(2, p, b1p, b2) for p in (0, 1)]

    z_arrive(1, 0, f_own[0], f1)
    reorder(to_q, 0, f1, f1p)
    q_arrive(2, 0, q_exchange(2, 0, f1p, f2), f2)
    lane_tiles(step_mixed, LPARTS[0])
    mq0 = q_exchange(3, 0, mo, m1)
    lane_tiles(step_kernel, LPARTS[0])
    lane_tiles(step_right, LPARTS[0])
    q_arrive(3, 0, mq0, m1)
    reorder(to_z, 0, m1, m1p)
    z_bytes(0, b2, z_ss.at[4])
    z_part(1, 1, first, f1, ZORDER)

    half = S2 // 2
    rows_l = half // NC

    def left_rows(index, p):
        spot = pl.ds(pl.multiple_of(index * half, half), half)
        lanes = pl.ds(*LPARTS[p])
        return dot(b2[spot, lanes], tokens[:, lanes], ((1,), (1,)))

    z_arrive(2, 0, b_own[0], b2)
    left_give[...] = left_rows(1 - core, 0)
    left_half[...] = left_rows(core, 0)
    m_own = [z_own(3, 0, m1p, mixed_ref)]
    z_arrive(2, 1, b_own[1], b2)
    left_give[...] += left_rows(1 - core, 1)
    c1 = send(left_give, left_mate, s_ss.at[5], s_rs.at[5], mate)
    z_part(3, 0, m1p, mixed_ref, MPARTS[0])
    left_half[...] += left_rows(core, 1)
    c1.wait()
    left_half[...] += left_mate[...]
    for j, cc in enumerate(chip_peers):
        send(block(left_half, cc, rows_l), left_xy.at[j], s_ss.at[8], s_rs.at[8], at_chip(cc))

    def step_tokens(lanes):
        tgrad[:, lanes] = dot(left_ref[...], b2[:, lanes], ((0,), (0,))).astype(BF16)

    lane_tiles(step_tokens)
    save_tokens = pltpu.make_async_copy(tgrad, tgrad_ref, own_sem.at[20])
    save_tokens.start()

    z_arrive(1, 1, f_own[1], f1)
    reorder(to_q, 1, f1, f1p)
    fq1 = q_exchange(2, 1, f1p, f2)

    sum_l = left_half[pl.ds(pl.multiple_of(chip * rows_l, rows_l), rows_l), :]
    bytes_of(left_xy, s_ss.at[8])
    bytes_of(left_xy, s_rs.at[8])
    for j in range(NC - 1):
        sum_l = sum_l + left_xy[j]
    for n in range(NZ):
        z_send[n] = sum_l[n // 4 * 4 : n // 4 * 4 + 4, n % 4 * 128 : n % 4 * 128 + 128]
    z_recv[z] = z_send[z]
    for zz in z_peers:
        send(z_send.at[zz], z_recv.at[z], s_ss.at[9], s_rs.at[9], along_z(zz))
    z_part(3, 0, m1p, mixed_ref, MPARTS[1])

    q_arrive(2, 1, fq1, f2)
    lane_tiles(step_mixed, LPARTS[1])
    mq1 = q_exchange(3, 1, mo, m1)

    lane_tiles(step_kernel, LPARTS[1])
    by_block = dot(expand[...].astype(F32), ksum[...] * pick, ((0,), (0,)), lax.Precision.HIGHEST)
    k_local[...] = by_block.T[0:4, :]
    k1 = send(k_local, k_core, s_ss.at[1], s_rs.at[1], mate)

    lane_tiles(step_right, LPARTS[1])
    halves = dot(expand[...].astype(F32), pairs[...] * same, ((0,), (0,)), lax.Precision.HIGHEST)
    rights = dot(halves, expand[...].astype(F32), ((1,), (0,)), lax.Precision.HIGHEST)
    for n in range(2 * NC):
        right_local[n] = rights[4 * n : 4 * n + 4, :]
    for j, (there, n) in enumerate(plane_peers):
        send(right_local.at[n], right_xy.at[j], s_ss.at[6], s_rs.at[6], there)
    z_tiles = right_z.at[pl.ds(0, NZ - 1)]
    bytes_of(z_tiles, s_ss.at[9])
    bytes_of(z_tiles, s_rs.at[9])
    whole_l = z_recv[0]
    for n in range(1, NZ):
        whole_l = whole_l + z_recv[n]
    piece[...] = whole_l * LEFT_SCALE
    z_gather[z] = piece[...]
    for zz in z_peers:
        send(piece, z_gather.at[z], s_ss.at[11], s_rs.at[11], along_z(zz))

    z_part(3, 0, m1p, mixed_ref, MPARTS[2])
    k1.wait()
    k_half[...] = k_local[...] + k_core[...]
    k2 = send(k_half, k_hi, s_ss.at[2], s_rs.at[2], across)

    sum_r = right_local[number]
    bytes_of(right_xy, s_ss.at[6])
    bytes_of(right_xy, s_rs.at[6])
    for j in range(2 * NC - 1):
        sum_r = sum_r + right_xy[j]
    right_half[...] = sum_r
    right_z[z] = sum_r
    for zz in z_peers:
        send(right_half, right_z.at[z], s_ss.at[7], s_rs.at[7], along_z(zz))

    q_arrive(3, 1, mq1, m1)
    reorder(to_z, 1, m1, m1p)
    m_own.append(z_own(3, 1, m1p, mixed_ref))
    z_part(3, 1, m1p, mixed_ref, LASTPARTS[0])
    k2.wait()
    k_total[...] = (k_half[...] + k_hi[...]) * KERNEL_SCALE
    kernel_moved = move(k_total, k_home, 3, (dp, holder))
    z_part(3, 1, m1p, mixed_ref, LASTPARTS[1])

    bytes_of(z_tiles, s_ss.at[11])
    bytes_of(z_tiles, s_rs.at[11])
    for n in range(NZ):
        own_rows[n // 4 * 4 : n // 4 * 4 + 4, n % 4 * 128 : n % 4 * 128 + 128] = z_gather[n]
    lgrad[pl.ds(pl.multiple_of(core * half + chip * rows_l, rows_l), rows_l), :] = own_rows[...]

    def part_l(which, cc):
        return lgrad.at[pl.ds(pl.multiple_of(which * half + cc * rows_l, rows_l), rows_l)]

    mine = part_l(core, chip)
    lx = [send(mine, mine, x_ss.at[0], x_rs.at[j], at_chip(cc)) for j, cc in enumerate(chip_peers)]
    send(mine, mine, x_ss.at[1], s_rs.at[12], mate)

    bytes_of(z_tiles, s_ss.at[7])
    bytes_of(z_tiles, s_rs.at[7])
    whole_r = right_z[0]
    for n in range(1, NZ):
        whole_r = whole_r + right_z[n]
    right_piece[...] = whole_r * RIGHT_SCALE
    right_all[number] = right_piece[...]
    for there, n in plane_peers:
        send(right_piece, right_all.at[number], s_ss.at[10], s_rs.at[10], there)
    for j, cc in enumerate(chip_peers):
        lx[j].wait_recv()
        send(part_l(core, cc), part_l(core, cc), x_ss.at[1], s_rs.at[12], mate)
    bytes_of(left_xy, x_ss.at[0])
    bytes_of(lgrad.at[pl.ds(0, half)], x_ss.at[1])
    bytes_of(lgrad.at[pl.ds(0, half)], s_rs.at[12])
    save_left = pltpu.make_async_copy(lgrad, lgrad_ref, own_sem.at[24])
    save_left.start()
    kernel_moved()
    bytes_of(right_xy, s_ss.at[10])
    bytes_of(right_xy, s_rs.at[10])
    for n in range(2 * NC):
        rgrad[4 * n : 4 * n + 4, :] = right_all[n]
    saves = [
        pltpu.make_async_copy(src, dst, own_sem.at[22 + n])
        for n, (src, dst) in enumerate([(k_home, kgrad_ref), (rgrad, rgrad_ref)])
    ]
    for save in saves:
        save.start()
    save_tokens.wait()
    save_left.wait()
    for n, p, buffer in [(0, 1, g1), (1, 0, f1), (1, 1, f1), (2, 1, b2), (3, 0, m1p), (3, 1, m1p)]:
        z_bytes(p, buffer, z_ss.at[2 * n + p])
    for n, buffer in enumerate([g2, b1, f2, m1]):
        for p in (0, 1):
            q_bytes(p, buffer, q_ss.at[2 * n + p])
    for p in (0, 1):
        m_own[p].wait()
        z_bytes(p, m1p, z_rs.at[6 + p])
    for save in saves:
        save.wait()


def keep(*refs):
    pieces = []
    for n in range(5):
        rows = refs[n].shape[0]
        step = max(rows // KEEP_PARTS, 4) if rows == S2 else rows
        pieces += [(n, at, step) for at in range(0, rows, step)]
    load_sem, save_sem = refs[15], refs[16]
    loads, saves = [], []
    for i, (n, at, step) in enumerate(pieces):
        spot = pl.ds(at, step)
        loads.append(pltpu.make_async_copy(refs[n].at[spot], refs[10 + n].at[spot], load_sem.at[i]))
        saves.append(pltpu.make_async_copy(refs[10 + n].at[spot], refs[5 + n].at[spot], save_sem.at[i]))
        loads[-1].start()
    for load, save in zip(loads, saves):
        load.wait()
        save.start()
    for save in saves:
        save.wait()


def on_device(tokens, left_factor, right_factor, gate_kernel, out_grad):
    hbm = pl.BlockSpec(memory_space=pl.ANY)
    plane = pltpu.VMEM((S2, D), BF16)
    square = pltpu.VMEM((S2, S2), BF16)
    four = pltpu.VMEM((4, S1), F32)
    half = S2 // 2
    dma = pltpu.SemaphoreType.DMA
    results = (
        jax.ShapeDtypeStruct((S2, D), BF16),
        jax.ShapeDtypeStruct((S2, D), BF16),
        jax.ShapeDtypeStruct((S2, S2), F32),
        jax.ShapeDtypeStruct((S1, S1), F32),
        jax.ShapeDtypeStruct((4, S1), F32),
    )
    made = pl.pallas_call(
        kernel,
        name="monarch",
        out_shape=results,
        in_specs=[hbm] * 5,
        out_specs=(hbm,) * 5,
        scratch_shapes=[
            plane, plane, square, pltpu.VMEM((S1, S1), BF16),
            *[plane] * 12,
            pltpu.VMEM((S2, D), F32),
            *[plane] * 4,
            square, square, pltpu.VMEM((S2, S1), BF16), square, square,
            four, pltpu.VMEM((S2, S1), F32), pltpu.VMEM((S2, S1), F32),
            *[pltpu.VMEM((half, S2), F32)] * 3,
            pltpu.VMEM((NC - 1, half // NC, S2), F32),
            pltpu.VMEM((NZ, 4, S1), F32), pltpu.VMEM((NZ, 4, S1), F32), four, pltpu.VMEM((NZ, 4, S1), F32),
            pltpu.VMEM((half // NC, S2), F32),
            pltpu.VMEM((S2, S2), F32), pltpu.VMEM((S2, S2), F32), pltpu.VMEM((2 * NC, 4, S1), F32),
            pltpu.VMEM((2 * NC - 1, 4, S1), F32), four, pltpu.VMEM((NZ, 4, S1), F32), four,
            pltpu.VMEM((2 * NC, 4, S1), F32),
            pltpu.VMEM((S1, S1), F32),
            *[four] * 6,
            dma((4,)), dma((25,)), dma((8,)), dma((8,)), dma((8,)), dma((8,)),
            dma((14,)), dma((14,)), dma((2,)), dma((NC - 1,)),
        ],
        compiler_params=pltpu.CompilerParams(
            collective_id=0, has_side_effects=True, vmem_limit_bytes=VMEM_LIMIT
        ),
    )(tokens.reshape(S2, D), left_factor, right_factor, gate_kernel.T, out_grad.reshape(S2, D))
    mixed, tgrad, lgrad, rgrad, kgrad = pl.pallas_call(
        keep,
        name="keep",
        out_shape=results,
        in_specs=[hbm] * 5,
        out_specs=(hbm,) * 5,
        scratch_shapes=[
            *[pltpu.VMEM(result.shape, result.dtype) for result in results],
            dma((3 * KEEP_PARTS + 2,)), dma((3 * KEEP_PARTS + 2,)),
        ],
    )(*made)
    return mixed.reshape(tokens.shape), tgrad.reshape(tokens.shape), lgrad, rgrad, kgrad.T


def solution(mesh):
    blocks = P("dp", "seq", None, None)
    return jax.shard_map(
        on_device,
        mesh=mesh,
        in_specs=(blocks, P(), P(), P(None, "seq"), blocks),
        out_specs=(blocks, blocks, P(), P(), P(None, "seq")),
        check_vma=False,
    )
```
